32 devices in a mesh: groups: 2 (over y), dom: 4 (over z), sub: 2 (over x), chip: 2 (over core).
Axes of the slice: x: 2, y: 2, z: 4, core: 2. Of those that a mesh axis runs over, the one named last changes fastest.
Arguments:
- node_input: bfloat16 [32768, 128], P(('groups', 'dom', 'sub', 'chip')), parts along dimension 0, may hold values from -6 to 6
- fine_neighbours: int32 [8, 32768], P(None, ('groups', 'dom', 'sub', 'chip')), parts along dimension 1, may hold values from -128 to 128, as said below
- fine_edge_weight: float32 [8, 32768], P(None, ('groups', 'dom', 'sub', 'chip')), parts along dimension 1, may hold values from 0.05 to 0.5
- coarse_parent: int32 [32768], P(('groups', 'dom', 'sub', 'chip')), parts along dimension 0, may hold values from 0 to 8191, as said below
- restrict_weight: float32 [32768], P(('groups', 'dom', 'sub', 'chip')), parts along dimension 0, may hold values from 0.3 to 1
- prolong_weight: float32 [32768], P(('groups', 'dom', 'sub', 'chip')), parts along dimension 0, may hold values from 0.3 to 1
- coarse_neighbours: int32 [8, 16384], P(None, ('groups', 'dom', 'sub', 'chip')), parts along dimension 1, may hold values from -128 to 128, as said below
- coarse_edge_weight: float32 [8, 16384], P(None, ('groups', 'dom', 'sub', 'chip')), parts along dimension 1, may hold values from 0.05 to 0.5
- fine_target: float32 [4, 32768], P(None, ('groups', 'dom', 'sub', 'chip')), parts along dimension 1, may hold values from -6 to 6
- coarse_target: float32 [4, 16384], P(None, ('groups', 'dom', 'sub', 'chip')), parts along dimension 1, may hold values from -6 to 6
- proc_weight: bfloat16 [2, 3, 128, 128], replicated, may hold values from -0.5 to 0.5
- head_weight: bfloat16 [2, 4, 128], replicated, may hold values from -0.5 to 0.5
Outputs:
- input_grad: float32 [32768, 128], P(('groups', 'dom', 'sub', 'chip')), parts along dimension 0
- proc_grad: float32 [4, 3, 128, 128], P('groups'), parts along dimension 0
- head_grad: float32 [4, 4, 128], P('groups'), parts along dimension 0
The draws below stay inside these ranges and needn't reach their ends.
There are 2 independent parts, one for each index of `groups`. The reference program is written for one: setup_inputs(seed, part) draws one part's arguments, and reference() takes and returns one part's arrays. A program takes and returns all parts, laid end to end along the dimension named above; an argument that names none is the same for every part. Nothing has to cross between parts.
Inputs may be any that keep to these rules, and one draw needn't show every extreme that they name: `fine_neighbours`: node i + entry [k, i] is a fine node of the window. `coarse_neighbours`: node i + entry [k, i] is a coarse node of the window. `coarse_parent`: for fine node i with parent p: p // 512 % 4 == i // 1024 % 4. Among the fine nodes of one aligned block of 1024 rows, at most 512 have parents with the same p // 2048, and exactly 512 do for one value.
All inputs are finite; a program needn't handle non-finite values.
Results may differ from the reference program's by a relative error of at most 0.018.
Values may be sent and summed in bfloat16 or wider, within the bound.
A program may use at most 64 MiB of HBM per device.

```python
import math
import jax
import jax.numpy as jnp

C = 128
K = 8
REACH = 128
HEADS = 4
LEVELS = 2
R0 = 1024
RC = 512
PEERS = 4
DEVS = 16
CAP = 512
N0 = 16384
NC = 8192


def near_rows(key, row_count):
    offsets = jax.random.randint(key, (K, row_count), -REACH, REACH + 1)
    rows = jnp.arange(row_count, dtype=jnp.int32)[None, :]
    clipped = jnp.clip(rows + offsets, 0, row_count - 1)
    return (clipped - rows).astype(jnp.int32)


def draw_fine_neighbours(key, part):
    key = jax.random.fold_in(key, 21)
    return near_rows(key, N0)


def draw_coarse_neighbours(key, part):
    key = jax.random.fold_in(key, 22)
    return near_rows(key, NC)


def shuffle_block(block_key):
    return jax.random.permutation(block_key, R0)


def draw_coarse_parent(key, part):
    key = jax.random.fold_in(key, 23)
    hot_key, offset_key, order_key, row_key = jax.random.split(key, 4)
    domains = DEVS // PEERS
    others = max(domains - 1, 1)
    hottest = jax.random.randint(hot_key, (DEVS,), 0, domains)
    offset = jax.random.randint(offset_key, (DEVS,), 0, others)
    within = jnp.arange(R0)
    spread = (within[None, :] - CAP + offset[:, None]) % others
    elsewhere = (hottest[:, None] + 1 + spread) % domains
    target = jnp.where(within[None, :] < CAP, hottest[:, None], elsewhere)
    orders = jax.vmap(shuffle_block)(jax.random.split(order_key, DEVS))
    target = jnp.take_along_axis(target, orders, axis=1)
    lanes = jnp.arange(DEVS) % PEERS
    chosen = jax.random.randint(row_key, (DEVS, R0), 0, RC)
    parent = (target * PEERS + lanes[:, None]) * RC + chosen
    return parent.reshape(-1).astype(jnp.int32)


def steps_of(stream_key, shape, cuts, least, largest):
    loudness = 1.0
    for position, blocks in cuts:
        steps = jax.random.uniform(jax.random.fold_in(jax.random.fold_in(stream_key, 6), position), (blocks,), jnp.float32, least / len(cuts), largest / len(cuts))
        loudness = loudness * jnp.repeat(jnp.exp(steps), shape[position] // blocks).reshape((-1,) + (1,) * (len(shape) - 1 - position))
    return loudness


def bell_draw(key, extent, width, reach, shards=(), held_as=jnp.bfloat16):
    level = steps_of(key, extent, shards, -0.22, 0.18) if shards else 1.0
    drawn = jax.random.normal(key, extent, jnp.float32) * width * level
    return jnp.minimum(jnp.maximum(drawn, -reach), reach).astype(held_as)


def setup_inputs(seed: int = 0, part: int = 0) -> dict:
    splits = jax.random.split(jax.random.key(seed), 13)
    part_keys = jax.random.split(jax.random.fold_in(splits[12], part), 13)
    return {
        "node_input": bell_draw(part_keys[0], (N0, C), 1.0, 6.0, ((0, 16),)),
        "fine_neighbours": draw_fine_neighbours(jax.random.fold_in(jax.random.fold_in(splits[12], part), 71), part),
        "fine_edge_weight": jnp.clip(jnp.exp(math.log(0.5) - 2.3025851 * jax.random.uniform(part_keys[2], (K, N0), jnp.float32) ** steps_of(part_keys[2], (K, N0), ((1, 16),), -0.2, 0.2)), 0.05, 0.5),
        "coarse_parent": draw_coarse_parent(jax.random.fold_in(jax.random.fold_in(splits[12], part), 71), part),
        "restrict_weight": jnp.clip(jnp.exp(math.log(1.0) - 1.2039728 * jax.random.uniform(part_keys[4], (N0,), jnp.float32) ** steps_of(part_keys[4], (N0,), ((0, 16),), -0.2, 0.2)), 0.3, 1.0),
        "prolong_weight": jnp.clip(jnp.exp(math.log(1.0) - 1.2039728 * jax.random.uniform(part_keys[5], (N0,), jnp.float32) ** steps_of(part_keys[5], (N0,), ((0, 16),), -0.2, 0.2)), 0.3, 1.0),
        "coarse_neighbours": draw_coarse_neighbours(jax.random.fold_in(jax.random.fold_in(splits[12], part), 71), part),
        "coarse_edge_weight": jnp.clip(jnp.exp(math.log(0.5) - 2.3025851 * jax.random.uniform(part_keys[7], (K, NC), jnp.float32) ** steps_of(part_keys[7], (K, NC), ((1, 16),), -0.2, 0.2)), 0.05, 0.5),
        "fine_target": bell_draw(part_keys[8], (HEADS, N0), 1.0, 6.0, ((1, 16),), jnp.float32),
        "coarse_target": bell_draw(part_keys[9], (HEADS, NC), 1.0, 6.0, ((1, 16),), jnp.float32),
        "proc_weight": bell_draw(splits[10], (LEVELS, 3, C, C), C ** -0.5, 0.5),
        "head_weight": bell_draw(splits[11], (LEVELS, HEADS, C), C ** -0.5, 0.5),
    }


def silu_slope(preact):
    sigma = jax.nn.sigmoid(preact)
    return sigma * (1.0 + preact * (1.0 - sigma))


def absolute_rows(neighbours):
    return jnp.arange(neighbours.shape[1], dtype=jnp.int32)[None, :] + neighbours.astype(jnp.int32)


def layer_forward(feature, neighbours, edge_weight, weights):
    targets = absolute_rows(neighbours)
    summed = jnp.zeros(feature.shape, jnp.float32)
    for neighbour in range(K):
        summed = summed + edge_weight[neighbour][:, None] * feature[targets[neighbour]].astype(jnp.float32)
    aggregate = summed.astype(jnp.bfloat16)
    preact = jnp.dot(feature, weights[0], preferred_element_type=jnp.float32) + jnp.dot(aggregate, weights[1], preferred_element_type=jnp.float32)
    active = jax.nn.silu(preact).astype(jnp.bfloat16)
    output = (feature.astype(jnp.float32) + jnp.dot(active, weights[2], preferred_element_type=jnp.float32)).astype(jnp.bfloat16)
    return output, aggregate, preact, active


def layer_backward(feature, aggregate, preact, active, neighbours, edge_weight, weights, upstream):
    targets = absolute_rows(neighbours)
    grad_pre = (jnp.dot(upstream, weights[2].T, preferred_element_type=jnp.float32) * silu_slope(preact)).astype(jnp.bfloat16)
    grad_wa = jnp.dot(feature.T, grad_pre, preferred_element_type=jnp.float32)
    grad_wb = jnp.dot(aggregate.T, grad_pre, preferred_element_type=jnp.float32)
    grad_wc = jnp.dot(active.T, upstream, preferred_element_type=jnp.float32)
    grad_agg = jnp.dot(grad_pre, weights[1].T, preferred_element_type=jnp.float32).astype(jnp.bfloat16)
    spread = jnp.zeros(feature.shape, jnp.float32)
    for neighbour in range(K):
        spread = spread.at[targets[neighbour]].add(edge_weight[neighbour][:, None] * grad_agg.astype(jnp.float32))
    grad_feature = upstream.astype(jnp.float32) + jnp.dot(grad_pre, weights[0].T, preferred_element_type=jnp.float32) + spread
    return grad_feature, jnp.stack([grad_wa, grad_wb, grad_wc])


def reference(node_input, fine_neighbours, fine_edge_weight, coarse_parent, restrict_weight, prolong_weight, coarse_neighbours, coarse_edge_weight, fine_target, coarse_target, proc_weight, head_weight):
    fine_out, fine_agg, fine_pre, fine_act = layer_forward(node_input, fine_neighbours, fine_edge_weight, proc_weight[0])
    contrib = (restrict_weight[:, None] * fine_out.astype(jnp.float32)).astype(jnp.bfloat16)
    coarse_in = jnp.zeros((NC, fine_out.shape[1]), jnp.float32).at[coarse_parent].add(contrib.astype(jnp.float32)).astype(jnp.bfloat16)
    coarse_out, coarse_agg, coarse_pre, coarse_act = layer_forward(coarse_in, coarse_neighbours, coarse_edge_weight, proc_weight[1])
    joined = (fine_out.astype(jnp.float32) + prolong_weight[:, None] * coarse_out[coarse_parent].astype(jnp.float32)).astype(jnp.bfloat16)
    fine_err = jnp.dot(head_weight[0], joined.T, preferred_element_type=jnp.float32) - fine_target
    coarse_err = jnp.dot(head_weight[1], coarse_out.T, preferred_element_type=jnp.float32) - coarse_target
    fine_errb = fine_err.astype(jnp.bfloat16)
    coarse_errb = coarse_err.astype(jnp.bfloat16)
    head_fine = jnp.dot(fine_errb, joined, preferred_element_type=jnp.float32)
    head_coarse = jnp.dot(coarse_errb, coarse_out, preferred_element_type=jnp.float32)
    grad_joined = jnp.dot(fine_errb.T, head_weight[0], preferred_element_type=jnp.float32).astype(jnp.bfloat16)
    pushed = (prolong_weight[:, None] * grad_joined.astype(jnp.float32)).astype(jnp.bfloat16)
    coarse_up = jnp.dot(coarse_errb.T, head_weight[1], preferred_element_type=jnp.float32)
    coarse_up = coarse_up.at[coarse_parent].add(pushed.astype(jnp.float32)).astype(jnp.bfloat16)
    coarse_grad, coarse_terms = layer_backward(coarse_in, coarse_agg, coarse_pre, coarse_act, coarse_neighbours, coarse_edge_weight, proc_weight[1], coarse_up)
    coarse_gradb = coarse_grad.astype(jnp.bfloat16)
    fine_up = (grad_joined.astype(jnp.float32) + restrict_weight[:, None] * coarse_gradb[coarse_parent].astype(jnp.float32)).astype(jnp.bfloat16)
    input_grad, fine_terms = layer_backward(node_input, fine_agg, fine_pre, fine_act, fine_neighbours, fine_edge_weight, proc_weight[0], fine_up)
    inverse_count = 1.0 / N0
    proc_grad = jnp.stack([fine_terms, coarse_terms]) * inverse_count
    head_grad = jnp.stack([head_fine, head_coarse]) * inverse_count
    return input_grad, proc_grad, head_grad
```

```python
import functools

import jax
import jax.numpy as jnp
from jax import lax
from jax.experimental import pallas as pl
from jax.experimental.pallas import tpu as pltpu
from jax.sharding import PartitionSpec as P

REACH = 128
MESH = pl.DeviceIdType.MESH
BF = jnp.bfloat16
F32 = jnp.float32


def dot(a, b):
    return jnp.dot(a, b, preferred_element_type=F32)


def dot_nt(a, b):
    return lax.dot_general(a, b, (((1,), (1,)), ((), ())), preferred_element_type=F32)


def dot_tn(a, b):
    return lax.dot_general(a, b, (((0,), (0,)), ((), ())), preferred_element_type=F32)


def build_band(nb_ref, ew_ref, band):
    base = lax.broadcasted_iota(jnp.int32, (3 * REACH, REACH), 0) - lax.broadcasted_iota(
        jnp.int32, (3 * REACH, REACH), 1
    )

    def body(b, carry):
        lanes = pl.ds(pl.multiple_of(b * REACH, REACH), REACH)
        total = jnp.zeros((3 * REACH, REACH), F32)
        for k in range(nb_ref.shape[0]):
            hit = base == nb_ref[k : k + 1, lanes] + REACH
            total = total + jnp.where(hit, ew_ref[k : k + 1, lanes], 0.0)
        band[b] = total.astype(BF)
        return carry

    lax.fori_loop(0, band.shape[0], body, 0)


def forward(ext, band, agg, act, slope, weights):
    blocks = band.shape[0]
    for b in range(blocks):
        agg[:, b * REACH : (b + 1) * REACH] = dot(
            ext[:, b * REACH : (b + 3) * REACH], band[b]
        ).astype(BF)
    feature = ext[:, REACH : (blocks + 1) * REACH]
    pre = dot_tn(weights[0], feature) + dot_tn(weights[1], agg[...])
    sigma = jax.nn.sigmoid(pre)
    act[...] = (pre * sigma).astype(BF)
    slope[...] = sigma * (1.0 + pre * (1.0 - sigma))
    return (feature.astype(F32) + dot_tn(weights[2], act[...])).astype(BF)


def kernel(
    dims,
    x_ref,
    fnb_ref,
    few_ref,
    parent_ref,
    restrict_ref,
    prolong_ref,
    cnb_ref,
    cew_ref,
    ft_ref,
    ct_ref,
    w_ref,
    head_ref,
    gin_ref,
    proc_ref,
    hgrad_ref,
    band_f,
    band_c,
    slots,
    pool_r,
    pool_p,
    ext_f,
    ext_c,
    halo_f,
    halo_c_out,
    halo_c,
    rim_f_out,
    rim_f,
    rim_c_out,
    rim_c,
    extra,
    extra_out,
    extra_in,
    slot_out,
    slot_in,
    back_out,
    back_in,
    joined_g,
    agg_f,
    act_f,
    slope_f,
    agg_c,
    act_c,
    slope_c,
    spread,
    gz_ref,
    up_f,
    up_c,
    acc,
    head8,
    gsum,
    ga_out,
    ga_in,
    gb_out,
    gb_in,
    gc_out,
    gc_in,
    gd_in,
    ring_send,
    ring_recv,
    dom_send,
    dom_recv,
    lane_send,
    lane_recv,
):
    D, S, H = dims
    L = S * H
    window = D * L
    rows = x_ref.shape[0]
    coarse = ct_ref.shape[1]
    nblk, blk = slots.shape[0], slots.shape[1]
    cpb = nblk // D
    cap = cpb * blk
    grp = lax.axis_index("groups")
    dom = lax.axis_index("dom")
    sub = lax.axis_index("sub")
    chip = lax.axis_index("chip")
    lane = sub * H + chip
    me = dom * L + lane

    def at_pos(p):
        return (grp, p // L, (p % L) // H, p % H)

    def at_dom(d):
        return (grp, d, sub, chip)

    def at_lane(q):
        return (grp, dom, q // H, q % H)

    left = at_pos((me + window - 1) % window)
    right = at_pos((me + 1) % window)

    barrier = pltpu.get_barrier_semaphore()
    peers = [left, right]
    peers += [at_dom((dom + o) % D) for o in range(1, D)]
    peers += [at_lane((lane + o) % L) for o in range(1, L)]
    for peer in peers:
        pl.semaphore_signal(barrier, inc=1, device_id=peer, device_id_type=MESH)
    pl.semaphore_wait(barrier, len(peers))

    started = []

    def send(src, dst, ssem, rsem, device):
        copy = pltpu.make_async_remote_copy(
            src_ref=src, dst_ref=dst, send_sem=ssem, recv_sem=rsem, device_id=device, device_id_type=MESH
        )
        copy.start()
        started.append(copy)

    def arrive(dst, ssem, rsem, device):
        pltpu.make_async_remote_copy(
            src_ref=dst, dst_ref=dst, send_sem=ssem, recv_sem=rsem, device_id=device, device_id_type=MESH
        ).wait_recv()

    def ring_start(stage, to_left, to_right, landing):
        send(to_right, landing.at[0], ring_send.at[stage, 0], ring_recv.at[stage, 0], right)
        send(to_left, landing.at[1], ring_send.at[stage, 1], ring_recv.at[stage, 1], left)

    def ring_wait(stage, landing):
        arrive(landing.at[0], ring_send.at[stage, 0], ring_recv.at[stage, 0], right)
        arrive(landing.at[1], ring_send.at[stage, 1], ring_recv.at[stage, 1], left)

    def dom_start(stage, off, src, dst):
        send(
            src, dst, dom_send.at[stage, off], dom_recv.at[stage, off], at_dom((dom + off) % D)
        )

    def dom_wait(stage, off, dst):
        arrive(dst, dom_send.at[stage, off], dom_recv.at[stage, off], at_dom((dom + off) % D))

    def part(d):
        return pl.ds(d * cpb, cpb)

    ring_start(0, x_ref.at[pl.ds(0, REACH)], x_ref.at[pl.ds(rows - REACH, REACH)], halo_f)

    parent = parent_ref[...]
    target = parent >> ((coarse * L).bit_length() - 1)
    local_row = parent & (coarse - 1)
    dpad = max(D, 16)
    onehot = (
        jnp.broadcast_to(target, (dpad, rows))
        == lax.broadcasted_iota(jnp.int32, (dpad, rows), 0)
    )
    onehot_f = jnp.where(onehot, 1.0, 0.0)
    upper = jnp.where(
        lax.broadcasted_iota(jnp.int32, (REACH, REACH), 0)
        <= lax.broadcasted_iota(jnp.int32, (REACH, REACH), 1),
        1.0,
        0.0,
    ).astype(BF)
    carry = jnp.zeros((dpad, 1), F32)
    within = []
    for b in range(rows // REACH):
        piece = onehot_f[:, b * REACH : (b + 1) * REACH]
        running = dot(piece.astype(BF), upper) + carry
        carry = carry + jnp.sum(piece, axis=1, keepdims=True)
        within.append(jnp.sum(piece * (running - 1.0), axis=0, keepdims=True))
    position = target * cap + jnp.concatenate(within, axis=1).astype(jnp.int32)

    extra[...] = jnp.zeros(extra.shape, F32)
    extra[0:4, :] = ft_ref[...]
    extra[4:5, :] = (local_row + 1).astype(F32)
    extra[5:6, :] = restrict_ref[...]
    extra[6:7, :] = prolong_ref[...]
    whole = extra[...]
    high = whole.astype(BF)
    rest = whole - high.astype(F32)
    middle = rest.astype(BF)
    low = (rest - middle.astype(F32)).astype(BF)
    slot_iota = lax.broadcasted_iota(jnp.int32, (blk, rows), 0)

    def slot_body(b, c):
        chosen = jnp.where(slot_iota == position - b * blk, 1.0, 0.0).astype(BF)
        slots[b] = chosen
        extra_out[b] = (dot_nt(high, chosen) + dot_nt(middle, chosen)) + dot_nt(low, chosen)
        return c

    lax.fori_loop(0, nblk, slot_body, 0)
    for off in range(1, D):
        dom_start(0, off, extra_out.at[part((dom + off) % D)], extra_in.at[part(dom)])
    extra_in[part(dom)] = extra_out[part(dom)]

    build_band(fnb_ref, few_ref, band_f)
    build_band(cnb_ref, cew_ref, band_c)
    head8[...] = jnp.zeros(head8.shape, F32)
    head8[0, 0:4, :] = head_ref[0].astype(F32)
    head8[1, 0:4, :] = head_ref[1].astype(F32)
    head_f = head8[0].astype(BF)
    head_c = head8[1].astype(BF)
    w_f = [w_ref[0, m] for m in range(3)]
    w_c = [w_ref[1, m] for m in range(3)]

    def turn(a):
        return jnp.transpose(a.astype(F32), (1, 0)).astype(BF)

    ext_f[:, REACH : REACH + rows] = turn(x_ref[...])
    ring_wait(0, halo_f)
    ext_f[:, 0:REACH] = turn(halo_f[0])
    ext_f[:, REACH + rows :] = turn(halo_f[1])
    out_f = forward(ext_f, band_f, agg_f, act_f, slope_f, w_f)

    for off in list(range(1, D)) + [0]:
        d = (dom + off) % D
        for c in range(cpb):
            b = d * cpb + c
            moved = dot_nt(out_f, slots[b]).astype(BF)
            if off:
                slot_out[b] = moved
            else:
                slot_in[b] = moved
        if off:
            dom_start(1, off, slot_out.at[part(d)], slot_in.at[part(dom)])

    for off in range(1, D):
        dom_wait(0, off, extra_in.at[part((dom + D - off) % D)])
    row_iota = lax.broadcasted_iota(jnp.int32, (coarse, blk), 0)

    def pool_body(b, c):
        info = extra_in[b]
        hit = row_iota == info[4:5, :].astype(jnp.int32) - 1
        pool_r[b] = jnp.where(hit, info[5:6, :], 0.0).astype(BF)
        pool_p[b] = jnp.where(hit, info[6:7, :], 0.0).astype(BF)
        return c

    lax.fori_loop(0, nblk, pool_body, 0)

    acc[...] = jnp.zeros(acc.shape, F32)
    for off in range(D):
        d = (dom + D - off) % D
        if off:
            dom_wait(1, off, slot_in.at[part(d)])
        for c in range(cpb):
            b = d * cpb + c
            acc[...] += dot_nt(slot_in[b], pool_r[b])
    ext_c[:, REACH : REACH + coarse] = acc[...].astype(BF)
    halo_c_out[0] = ext_c[:, REACH : 2 * REACH]
    halo_c_out[1] = ext_c[:, coarse : coarse + REACH]
    ring_start(1, halo_c_out.at[0], halo_c_out.at[1], halo_c)
    ring_wait(1, halo_c)
    ext_c[:, 0:REACH] = halo_c[0]
    ext_c[:, REACH + coarse :] = halo_c[1]
    out_c = forward(ext_c, band_c, agg_c, act_c, slope_c, w_c)

    top = lax.broadcasted_iota(jnp.int32, (8, blk), 0) < 4
    extra[:, 0:coarse] = jnp.zeros((8, coarse), F32)
    extra[0:4, 0:coarse] = ct_ref[...]
    errb_c = (dot(head_c, out_c) - extra[:, 0:coarse]).astype(BF)
    proc_rows = 6 * REACH
    gsum[proc_rows + 16 :] = jnp.zeros((gsum.shape[0] - proc_rows - 16, REACH), F32)
    gsum[proc_rows + 8 : proc_rows + 16] = dot_nt(errb_c, out_c)
    acc[...] = dot_tn(head_c, errb_c)

    def join_body(b, terms):
        joined = (slot_in[b].astype(F32) + dot(out_c, pool_p[b])).astype(BF)
        errb = (dot(head_f, joined) - jnp.where(top, extra_in[b], 0.0)).astype(BF)
        grad = dot_tn(head_f, errb).astype(BF)
        joined_g[b] = grad
        acc[...] += dot_nt(grad, pool_p[b])
        return terms + dot_nt(errb, joined)

    head_terms_f = lax.fori_loop(0, nblk, join_body, jnp.zeros((8, x_ref.shape[1]), F32))

    gsum[proc_rows : proc_rows + 8] = head_terms_f

    def backward(stage, up, band, agg, act, slope, feature, weights, rim_out, rim, level):
        blocks = band.shape[0]
        count = blocks * REACH
        gz = (dot(weights[2], up[...]) * slope[...]).astype(BF)
        gagg = dot(weights[1], gz).astype(BF)
        rim_out[0] = dot_nt(gagg[:, 0:REACH], band[0, 0:REACH]).astype(BF)
        rim_out[1] = dot_nt(gagg[:, count - REACH :], band[blocks - 1, 2 * REACH :]).astype(BF)
        ring_start(stage, rim_out.at[0], rim_out.at[1], rim)
        at = level * 3 * REACH
        gz_ref[:, 0:count] = gz
        gsum[at : at + 3 * REACH] = jnp.zeros((3 * REACH, REACH), F32)

        def grad_body(c, carry):
            lanes = pl.ds(pl.multiple_of(c * 512, 512), 512)
            part_z = gz_ref[:, lanes]
            shifted = pl.ds(pl.multiple_of(c * 512 + REACH, REACH), 512)
            gsum[at : at + REACH] += dot_nt(feature[:, shifted], part_z)
            gsum[at + REACH : at + 2 * REACH] += dot_nt(agg[:, lanes], part_z)
            gsum[at + 2 * REACH : at + 3 * REACH] += dot_nt(act[:, lanes], up[:, lanes])
            return carry

        lax.fori_loop(0, count // 512, grad_body, 0)
        grad = up[...].astype(F32) + dot(weights[0], gz)
        for b in range(blocks):
            lo, hi = max(b - 1, 0), min(b + 2, blocks)
            piece = dot_nt(
                gagg[:, b * REACH : (b + 1) * REACH],
                band[b, (lo - b + 1) * REACH : (hi - b + 1) * REACH],
            )
            if b == 0:
                spread[:, 0:count] = grad
            spread[:, lo * REACH : hi * REACH] += piece

    up_c[...] = acc[...].astype(BF)
    backward(
        2, up_c, band_c, agg_c, act_c, slope_c, ext_c, w_c, rim_c_out, rim_c, 1
    )
    ring_wait(2, rim_c)
    spread[:, 0:REACH] += rim_c[0].astype(F32)
    spread[:, coarse - REACH : coarse] += rim_c[1].astype(F32)
    grad_c = spread[:, 0:coarse].astype(BF)

    for off in list(range(1, D)) + [0]:
        d = (dom + off) % D
        for c in range(cpb):
            b = d * cpb + c
            moved = (joined_g[b].astype(F32) + dot(grad_c, pool_r[b])).astype(BF)
            if off:
                back_out[b] = moved
            else:
                back_in[b] = moved
        if off:
            dom_start(2, off, back_out.at[part(d)], back_in.at[part(dom)])

    spread[...] = jnp.zeros(spread.shape, F32)
    for off in range(D):
        d = (dom + D - off) % D
        if off:
            dom_wait(2, off, back_in.at[part(d)])
        for c in range(cpb):
            b = d * cpb + c
            spread[...] += dot(back_in[b], slots[b])
    up_f[...] = spread[...].astype(BF)
    backward(
        3, up_f, band_f, agg_f, act_f, slope_f, ext_f, w_f, rim_f_out, rim_f, 0
    )

    per_lane = ga_out.shape[1]
    per_dom = gb_out.shape[1]
    for q in range(L):
        ga_out[q] = gsum[q * per_lane : (q + 1) * per_lane].astype(BF)
    for off in range(1, L):
        send(
            ga_out.at[(lane + off) % L],
            ga_in.at[lane],
            lane_send.at[0, off],
            lane_recv.at[0, off],
            at_lane((lane + off) % L),
        )

    ring_wait(3, rim_f)
    spread[:, 0:REACH] += rim_f[0].astype(F32)
    spread[:, rows - REACH :] += rim_f[1].astype(F32)
    gin_ref[...] = jnp.transpose(spread[...], (1, 0))

    total = ga_out[lane].astype(F32)
    for off in range(1, L):
        q = (lane + L - off) % L
        arrive(ga_in.at[q], lane_send.at[0, off], lane_recv.at[0, off], at_lane((lane + off) % L))
        total = total + ga_in[q].astype(F32)
    for d in range(D):
        gb_out[d] = total[d * per_dom : (d + 1) * per_dom].astype(BF)
    for off in range(1, D):
        dom_start(3, off, gb_out.at[(dom + off) % D], gb_in.at[dom])
    mine = gb_out[dom].astype(F32)
    for off in range(1, D):
        d = (dom + D - off) % D
        dom_wait(3, off, gb_in.at[d])
        mine = mine + gb_in[d].astype(F32)
    gc_out[...] = mine.astype(BF)
    for off in range(1, D):
        dom_start(4, off, gc_out, gc_in.at[dom])
    gc_in[dom] = gc_out[...]
    for off in range(1, D):
        dom_wait(4, off, gc_in.at[(dom + D - off) % D])
    for off in range(1, L):
        send(
            gc_in,
            gd_in.at[lane],
            lane_send.at[1, off],
            lane_recv.at[1, off],
            at_lane((lane + off) % L),
        )
    gd_in[lane] = gc_in[...]
    for off in range(1, L):
        arrive(
            gd_in.at[(lane + L - off) % L],
            lane_send.at[1, off],
            lane_recv.at[1, off],
            at_lane((lane + off) % L),
        )
    scale = 1.0 / (rows * window)
    gsum[...] = gd_in[...].astype(F32).reshape(gsum.shape) * scale
    for m in range(6):
        proc_ref[m // 3, m % 3] = gsum[m * REACH : (m + 1) * REACH]
    hgrad_ref[0] = gsum[proc_rows : proc_rows + 4]
    hgrad_ref[1] = gsum[proc_rows + 8 : proc_rows + 12]
    for copy in started:
        copy.wait_send()


def per_device(dims, node_input, fnb, few, parent, restrict, prolong, cnb, cew, ft, ct, w, head):
    D, S, H = dims
    L = S * H
    rows, width = node_input.shape
    coarse = ct.shape[1]
    cap = 2 * rows // D
    blk = min(256, cap)
    nblk = 2 * rows // blk
    unit = 16 * L * D
    total = -(-(6 * REACH + 16) // unit) * unit
    fb, cb = rows // REACH, coarse // REACH
    vm = pltpu.VMEM
    scratch = [
        vm((fb, 3 * REACH, REACH), BF),
        vm((cb, 3 * REACH, REACH), BF),
        vm((nblk, blk, rows), BF),
        vm((nblk, coarse, blk), BF),
        vm((nblk, coarse, blk), BF),
        vm((width, rows + 2 * REACH), BF),
        vm((width, coarse + 2 * REACH), BF),
        vm((2, REACH, width), BF),
        vm((2, width, REACH), BF),
        vm((2, width, REACH), BF),
        vm((2, width, REACH), BF),
        vm((2, width, REACH), BF),
        vm((2, width, REACH), BF),
        vm((2, width, REACH), BF),
        vm((8, rows), F32),
        vm((nblk, 8, blk), F32),
        vm((nblk, 8, blk), F32),
        vm((nblk, width, blk), BF),
        vm((nblk, width, blk), BF),
        vm((nblk, width, blk), BF),
        vm((nblk, width, blk), BF),
        vm((nblk, width, blk), BF),
        vm((width, rows), BF),
        vm((width, rows), BF),
        vm((width, rows), F32),
        vm((width, coarse), BF),
        vm((width, coarse), BF),
        vm((width, coarse), F32),
        vm((width, rows), F32),
        vm((width, rows), BF),
        vm((width, rows), BF),
        vm((width, coarse), BF),
        vm((width, coarse), F32),
        vm((2, 8, width), F32),
        vm((total, width), F32),
        vm((L, total // L, width), BF),
        vm((L, total // L, width), BF),
        vm((D, total // L // D, width), BF),
        vm((D, total // L // D, width), BF),
        vm((total // L // D, width), BF),
        vm((D, total // L // D, width), BF),
        vm((L, D, total // L // D, width), BF),
        pltpu.SemaphoreType.DMA((4, 2)),
        pltpu.SemaphoreType.DMA((4, 2)),
        pltpu.SemaphoreType.DMA((5, D)),
        pltpu.SemaphoreType.DMA((5, D)),
        pltpu.SemaphoreType.DMA((2, L)),
        pltpu.SemaphoreType.DMA((2, L)),
    ]
    spec = pl.BlockSpec(memory_space=pltpu.VMEM)
    return pl.pallas_call(
        functools.partial(kernel, dims),
        out_shape=(
            jax.ShapeDtypeStruct((rows, width), F32),
            jax.ShapeDtypeStruct((2, 3, width, width), F32),
            jax.ShapeDtypeStruct((2, 4, width), F32),
        ),
        in_specs=[spec] * 12,
        out_specs=(spec, spec, spec),
        scratch_shapes=scratch,
        compiler_params=pltpu.CompilerParams(
            collective_id=0, has_side_effects=True, vmem_limit_bytes=50 * 1024 * 1024
        ),
    )(
        node_input,
        fnb,
        few,
        parent.reshape(1, rows),
        restrict.reshape(1, rows),
        prolong.reshape(1, rows),
        cnb,
        cew,
        ft,
        ct,
        w,
        head,
    )


def solution(mesh):
    dims = (mesh.shape["dom"], mesh.shape["sub"], mesh.shape["chip"])
    nodes = ("groups", "dom", "sub", "chip")
    return jax.shard_map(
        functools.partial(per_device, dims),
        mesh=mesh,
        in_specs=(
            P(nodes, None),
            P(None, nodes),
            P(None, nodes),
            P(nodes),
            P(nodes),
            P(nodes),
            P(None, nodes),
            P(None, nodes),
            P(None, nodes),
            P(None, nodes),
            P(),
            P(),
        ),
        out_specs=(
            P(nodes, None),
            P("groups", None, None, None),
            P("groups", None, None),
        ),
        check_vma=False,
    )
```

```python
import functools

import jax
import jax.numpy as jnp
from jax import lax
from jax.experimental import pallas as pl
from jax.experimental.pallas import tpu as pltpu
from jax.sharding import PartitionSpec as P

REACH = 128
MESH = pl.DeviceIdType.MESH
BF = jnp.bfloat16
F32 = jnp.float32


def dot(a, b):
    return jnp.dot(a, b, preferred_element_type=F32)


def dot_nt(a, b):
    return lax.dot_general(a, b, (((1,), (1,)), ((), ())), preferred_element_type=F32)


def dot_tn(a, b):
    return lax.dot_general(a, b, (((0,), (0,)), ((), ())), preferred_element_type=F32)


def build_band(nb_ref, ew_ref, band):
    base = lax.broadcasted_iota(jnp.int32, (3 * REACH, REACH), 0) - lax.broadcasted_iota(
        jnp.int32, (3 * REACH, REACH), 1
    )

    def body(b, carry):
        lanes = pl.ds(pl.multiple_of(b * REACH, REACH), REACH)
        total = jnp.zeros((3 * REACH, REACH), F32)
        for k in range(nb_ref.shape[0]):
            hit = base == nb_ref[k : k + 1, lanes] + REACH
            total = total + jnp.where(hit, ew_ref[k : k + 1, lanes], 0.0)
        band[b] = total.astype(BF)
        return carry

    lax.fori_loop(0, band.shape[0], body, 0)


def forward(ext, band, agg, act, slope, weights):
    blocks = band.shape[0]
    for b in range(blocks):
        agg[:, b * REACH : (b + 1) * REACH] = dot(
            ext[:, b * REACH : (b + 3) * REACH], band[b]
        ).astype(BF)
    feature = ext[:, REACH : (blocks + 1) * REACH]
    pre = dot_tn(weights[0], feature) + dot_tn(weights[1], agg[...])
    sigma = jax.nn.sigmoid(pre)
    act[...] = (pre * sigma).astype(BF)
    slope[...] = sigma * (1.0 + pre * (1.0 - sigma))
    return (feature.astype(F32) + dot_tn(weights[2], act[...])).astype(BF)


def entry(dims, *refs):
    held, local = refs[:12], refs[15:27]
    copies = [
        pltpu.make_async_copy(source, place, refs[27].at[i])
        for i, (source, place) in enumerate(zip(held, local))
    ]
    for i in (3, 4, 5, 8, 1, 2, 0, 6, 7, 10, 11, 9):
        copies[i].start()
    kernel(dims, copies, held[0], *local, *refs[12:15], *refs[28:])


def kernel(
    dims,
    copies,
    x_hbm,
    x_ref,
    fnb_ref,
    few_ref,
    parent_ref,
    restrict_ref,
    prolong_ref,
    cnb_ref,
    cew_ref,
    ft_ref,
    ct_ref,
    w_ref,
    head_ref,
    gin_ref,
    proc_ref,
    hgrad_ref,
    band_f,
    band_c,
    slots,
    pool_r,
    pool_p,
    ext_f,
    ext_c,
    halo_f,
    halo_c_out,
    halo_c,
    rim_f_out,
    rim_f,
    rim_c_out,
    rim_c,
    extra,
    extra_out,
    extra_in,
    slot_out,
    slot_in,
    back_out,
    back_in,
    joined_g,
    agg_f,
    act_f,
    slope_f,
    agg_c,
    act_c,
    slope_c,
    spread,
    gz_ref,
    up_f,
    up_c,
    acc,
    head8,
    gsum_f,
    a_out_f,
    a_in_f,
    b_in_f,
    d_in_f,
    gsum_c,
    a_out_c,
    a_in_c,
    b_in_c,
    d_in_c,
    ring_send,
    ring_recv,
    dom_send,
    dom_recv,
    lane_send,
    lane_recv,
):
    D, S, H = dims
    L = S * H
    window = D * L
    rows = x_ref.shape[0]
    coarse = ct_ref.shape[1]
    nblk, blk = slots.shape[0], slots.shape[1]
    cpb = nblk // D
    cap = cpb * blk
    grp = lax.axis_index("groups")
    dom = lax.axis_index("dom")
    sub = lax.axis_index("sub")
    chip = lax.axis_index("chip")
    lane = sub * H + chip
    me = dom * L + lane

    def at_pos(p):
        return (grp, p // L, (p % L) // H, p % H)

    def at_dom(d):
        return (grp, d, sub, chip)

    def at_lane(q):
        return (grp, dom, q // H, q % H)

    left = at_pos((me + window - 1) % window)
    right = at_pos((me + 1) % window)

    barrier = pltpu.get_barrier_semaphore()
    peers = [left, right]
    peers += [at_dom((dom + o) % D) for o in range(1, D)]
    peers += [at_lane((lane + o) % L) for o in range(1, L)]
    for peer in peers:
        pl.semaphore_signal(barrier, inc=1, device_id=peer, device_id_type=MESH)
    pl.semaphore_wait(barrier, len(peers))

    started = []

    def send(src, dst, ssem, rsem, device):
        copy = pltpu.make_async_remote_copy(
            src_ref=src, dst_ref=dst, send_sem=ssem, recv_sem=rsem, device_id=device, device_id_type=MESH
        )
        copy.start()
        started.append(copy)

    def arrive(dst, ssem, rsem, device):
        pltpu.make_async_remote_copy(
            src_ref=dst, dst_ref=dst, send_sem=ssem, recv_sem=rsem, device_id=device, device_id_type=MESH
        ).wait_recv()

    def ring_start(stage, to_left, to_right, landing):
        send(to_right, landing.at[0], ring_send.at[stage, 0], ring_recv.at[stage, 0], right)
        send(to_left, landing.at[1], ring_send.at[stage, 1], ring_recv.at[stage, 1], left)

    def ring_wait(stage, landing):
        arrive(landing.at[0], ring_send.at[stage, 0], ring_recv.at[stage, 0], right)
        arrive(landing.at[1], ring_send.at[stage, 1], ring_recv.at[stage, 1], left)

    arrivals = [0] + sorted(range(1, D), key=lambda o: (o & 1, o) if o != 1 else (0, D))
    order = sorted(range(1, D), key=lambda o: (-o.bit_length(), o))

    def mate(o):
        d = dom
        for k in range(o.bit_length()):
            if (o >> k) & 1:
                d = d + (1 - 2 * ((dom // 2**k) % 2)) * 2**k
        return d

    def dom_start(stage, o, src, dst):
        send(src, dst, dom_send.at[stage, o], dom_recv.at[stage, o], at_dom(mate(o)))

    def dom_wait(stage, o, dst):
        arrive(dst, dom_send.at[stage, o], dom_recv.at[stage, o], at_dom(mate(o)))

    def lane_start(stage, o, src, dst):
        send(src, dst, lane_send.at[stage, o], lane_recv.at[stage, o], at_lane((lane + o) % L))

    def lane_wait(stage, o, dst):
        arrive(dst, lane_send.at[stage, o], lane_recv.at[stage, o], at_lane((lane + o) % L))

    def sum_lanes(stage, source, a_out, a_in):
        share = a_out.shape[1]
        for q in range(L):
            a_out[q] = source[q * share : (q + 1) * share].astype(BF)
        for o in range(1, L):
            lane_start(stage, o, a_out.at[(lane + o) % L], a_in.at[lane])

    def sum_domains(stage, dom_stage, a_out, a_in, b_in):
        total = a_out[lane].astype(F32)
        for o in range(1, L):
            q = (lane + L - o) % L
            lane_wait(stage, o, a_in.at[q])
            total = total + a_in[q].astype(F32)
        b_in[dom] = total.astype(BF)
        for o in order:
            dom_start(dom_stage, o, b_in.at[dom], b_in.at[dom])

    def share_sums(stage, dom_stage, b_in, d_in):
        for o in order:
            dom_wait(dom_stage, o, b_in.at[mate(o)])
        total = b_in[0].astype(F32)
        for d in range(1, D):
            total = total + b_in[d].astype(F32)
        d_in[lane] = total.astype(BF)
        for o in range(1, L):
            lane_start(stage, o, d_in.at[lane], d_in.at[lane])

    def take_sums(stage, d_in, target):
        for o in range(1, L):
            lane_wait(stage, o, d_in.at[(lane + L - o) % L])
        target[...] = d_in[...].astype(F32).reshape(target.shape) * (1.0 / (rows * window))

    def part(d):
        return pl.ds(d * cpb, cpb)

    ring_start(0, x_hbm.at[pl.ds(0, REACH)], x_hbm.at[pl.ds(rows - REACH, REACH)], halo_f)

    for i in (3, 4, 5, 8):
        copies[i].wait()
    parent = parent_ref[...]
    target = parent >> ((coarse * L).bit_length() - 1)
    local_row = parent & (coarse - 1)
    dpad = max(D, 16)
    onehot = (
        jnp.broadcast_to(target, (dpad, rows))
        == lax.broadcasted_iota(jnp.int32, (dpad, rows), 0)
    )
    onehot_f = jnp.where(onehot, 1.0, 0.0)
    upper = jnp.where(
        lax.broadcasted_iota(jnp.int32, (REACH, REACH), 0)
        <= lax.broadcasted_iota(jnp.int32, (REACH, REACH), 1),
        1.0,
        0.0,
    ).astype(BF)
    carry = jnp.zeros((dpad, 1), F32)
    within = []
    for b in range(rows // REACH):
        piece = onehot_f[:, b * REACH : (b + 1) * REACH]
        running = dot(piece.astype(BF), upper) + carry
        carry = carry + jnp.sum(piece, axis=1, keepdims=True)
        within.append(jnp.sum(piece * (running - 1.0), axis=0, keepdims=True))
    position = target * cap + jnp.concatenate(within, axis=1).astype(jnp.int32)

    extra[...] = jnp.zeros(extra.shape, F32)
    extra[0:4, :] = ft_ref[...]
    extra[4:5, :] = (local_row + 1).astype(F32)
    extra[5:6, :] = restrict_ref[...]
    extra[6:7, :] = prolong_ref[...]
    whole = extra[...]
    high = whole.astype(BF)
    rest = whole - high.astype(F32)
    middle = rest.astype(BF)
    low = rest - middle.astype(F32)
    thirds = jnp.concatenate(
        [high.astype(F32), middle.astype(F32), low, jnp.zeros_like(low)], axis=0
    ).astype(BF)
    slot_iota = lax.broadcasted_iota(jnp.int32, (blk, rows), 0)

    def slot_body(b, c):
        chosen = jnp.where(slot_iota == position - b * blk, 1.0, 0.0).astype(BF)
        slots[b] = chosen
        found = dot_nt(thirds, chosen)
        extra_out[b] = found[0:8] + found[8:16] + found[16:24]
        return c

    lax.fori_loop(0, nblk, slot_body, 0)
    for o in order:
        dom_start(0, o, extra_out.at[part(mate(o))], extra_in.at[part(dom)])
    extra_in[part(dom)] = extra_out[part(dom)]

    for i in (1, 2, 0, 6, 7, 10, 11, 9):
        copies[i].wait()
    build_band(fnb_ref, few_ref, band_f)
    build_band(cnb_ref, cew_ref, band_c)
    head8[...] = jnp.zeros(head8.shape, F32)
    head8[0, 0:4, :] = head_ref[0].astype(F32)
    head8[1, 0:4, :] = head_ref[1].astype(F32)
    head_f = head8[0].astype(BF)
    head_c = head8[1].astype(BF)
    w_f = [w_ref[0, m] for m in range(3)]
    w_c = [w_ref[1, m] for m in range(3)]

    def turn(a):
        return jnp.transpose(a.astype(F32), (1, 0)).astype(BF)

    ext_f[:, REACH : REACH + rows] = turn(x_ref[...])
    ring_wait(0, halo_f)
    ext_f[:, 0:REACH] = turn(halo_f[0])
    ext_f[:, REACH + rows :] = turn(halo_f[1])
    out_f = forward(ext_f, band_f, agg_f, act_f, slope_f, w_f)

    for off in order + [0]:
        d = mate(off)
        for c in range(cpb):
            b = d * cpb + c
            moved = dot_nt(out_f, slots[b]).astype(BF)
            if off:
                slot_out[b] = moved
            else:
                slot_in[b] = moved
        if off:
            dom_start(1, off, slot_out.at[part(d)], slot_in.at[part(dom)])

    for o in order:
        dom_wait(0, o, extra_in.at[part(mate(o))])
    row_iota = lax.broadcasted_iota(jnp.int32, (coarse, blk), 0)

    def pool_body(b, c):
        info = extra_in[b]
        hit = row_iota == info[4:5, :].astype(jnp.int32) - 1
        pool_r[b] = jnp.where(hit, info[5:6, :], 0.0).astype(BF)
        pool_p[b] = jnp.where(hit, info[6:7, :], 0.0).astype(BF)
        return c

    lax.fori_loop(0, nblk, pool_body, 0)

    acc[...] = jnp.zeros(acc.shape, F32)
    for off in arrivals:
        d = mate(off)
        if off:
            dom_wait(1, off, slot_in.at[part(d)])
        for c in range(cpb):
            b = d * cpb + c
            acc[...] += dot_nt(slot_in[b], pool_r[b])
    ext_c[:, REACH : REACH + coarse] = acc[...].astype(BF)
    halo_c_out[0] = ext_c[:, REACH : 2 * REACH]
    halo_c_out[1] = ext_c[:, coarse : coarse + REACH]
    ring_start(1, halo_c_out.at[0], halo_c_out.at[1], halo_c)
    ring_wait(1, halo_c)
    ext_c[:, 0:REACH] = halo_c[0]
    ext_c[:, REACH + coarse :] = halo_c[1]
    out_c = forward(ext_c, band_c, agg_c, act_c, slope_c, w_c)

    top = lax.broadcasted_iota(jnp.int32, (8, blk), 0) < 4
    extra[:, 0:coarse] = jnp.zeros((8, coarse), F32)
    extra[0:4, 0:coarse] = ct_ref[...]
    errb_c = (dot(head_c, out_c) - extra[:, 0:coarse]).astype(BF)
    head_at = 3 * REACH
    if gsum_c.shape[0] > head_at + 16:
        gsum_c[head_at + 16 :] = jnp.zeros((gsum_c.shape[0] - head_at - 16, REACH), F32)
    gsum_c[head_at + 8 : head_at + 16] = dot_nt(errb_c, out_c)
    acc[...] = dot_tn(head_c, errb_c)

    def join_body(b, terms):
        joined = (slot_in[b].astype(F32) + dot(out_c, pool_p[b])).astype(BF)
        errb = (dot(head_f, joined) - jnp.where(top, extra_in[b], 0.0)).astype(BF)
        grad = dot_tn(head_f, errb).astype(BF)
        joined_g[b] = grad
        acc[...] += dot_nt(grad, pool_p[b])
        return terms + dot_nt(errb, joined)

    head_terms_f = lax.fori_loop(0, nblk, join_body, jnp.zeros((8, x_ref.shape[1]), F32))

    gsum_c[head_at : head_at + 8] = head_terms_f

    def backward(stage, up, band, agg, act, slope, feature, weights, rim_out, rim, gsum, then):
        blocks = band.shape[0]
        count = blocks * REACH
        gz = (dot(weights[2], up[...]) * slope[...]).astype(BF)
        gagg = dot(weights[1], gz).astype(BF)
        rim_out[0] = dot_nt(gagg[:, 0:REACH], band[0, 0:REACH]).astype(BF)
        rim_out[1] = dot_nt(gagg[:, count - REACH :], band[blocks - 1, 2 * REACH :]).astype(BF)
        ring_start(stage, rim_out.at[0], rim_out.at[1], rim)
        at = 0
        gz_ref[:, 0:count] = gz
        gsum[at : at + 3 * REACH] = jnp.zeros((3 * REACH, REACH), F32)

        def grad_body(c, carry):
            lanes = pl.ds(pl.multiple_of(c * 512, 512), 512)
            part_z = gz_ref[:, lanes]
            shifted = pl.ds(pl.multiple_of(c * 512 + REACH, REACH), 512)
            gsum[at : at + REACH] += dot_nt(feature[:, shifted], part_z)
            gsum[at + REACH : at + 2 * REACH] += dot_nt(agg[:, lanes], part_z)
            gsum[at + 2 * REACH : at + 3 * REACH] += dot_nt(act[:, lanes], up[:, lanes])
            return carry

        lax.fori_loop(0, count // 512, grad_body, 0)
        then()
        grad = up[...].astype(F32) + dot(weights[0], gz)
        for b in range(blocks):
            lo, hi = max(b - 1, 0), min(b + 2, blocks)
            piece = dot_nt(
                gagg[:, b * REACH : (b + 1) * REACH],
                band[b, (lo - b + 1) * REACH : (hi - b + 1) * REACH],
            )
            if b == 0:
                spread[:, 0:count] = grad
            spread[:, lo * REACH : hi * REACH] += piece

    up_c[...] = acc[...].astype(BF)
    backward(
        2, up_c, band_c, agg_c, act_c, slope_c, ext_c, w_c, rim_c_out, rim_c, gsum_c,
        lambda: sum_lanes(2, gsum_c, a_out_c, a_in_c),
    )
    ring_wait(2, rim_c)
    spread[:, 0:REACH] += rim_c[0].astype(F32)
    spread[:, coarse - REACH : coarse] += rim_c[1].astype(F32)
    grad_c = spread[:, 0:coarse].astype(BF)

    for off in order + [0]:
        d = mate(off)
        for c in range(cpb):
            b = d * cpb + c
            moved = (joined_g[b].astype(F32) + dot(grad_c, pool_r[b])).astype(BF)
            if off:
                back_out[b] = moved
            else:
                back_in[b] = moved
        if off:
            dom_start(2, off, back_out.at[part(d)], back_in.at[part(dom)])

    spread[...] = jnp.zeros(spread.shape, F32)
    for off in arrivals:
        d = mate(off)
        if off:
            dom_wait(2, off, back_in.at[part(d)])
        for c in range(cpb):
            b = d * cpb + c
            spread[...] += dot(back_in[b], slots[b])
    sum_domains(2, 4, a_out_c, a_in_c, b_in_c)
    up_f[...] = spread[...].astype(BF)
    if gsum_f.shape[0] > 3 * REACH:
        gsum_f[3 * REACH :] = jnp.zeros((gsum_f.shape[0] - 3 * REACH, REACH), F32)
    backward(
        3, up_f, band_f, agg_f, act_f, slope_f, ext_f, w_f, rim_f_out, rim_f, gsum_f,
        lambda: sum_lanes(0, gsum_f, a_out_f, a_in_f),
    )

    sum_domains(0, 3, a_out_f, a_in_f, b_in_f)
    share_sums(3, 4, b_in_c, d_in_c)
    ring_wait(3, rim_f)
    spread[:, 0:REACH] += rim_f[0].astype(F32)
    spread[:, rows - REACH :] += rim_f[1].astype(F32)
    gin_ref[...] = jnp.transpose(spread[...], (1, 0))
    share_sums(1, 3, b_in_f, d_in_f)
    take_sums(3, d_in_c, gsum_c)
    take_sums(1, d_in_f, gsum_f)
    for m in range(3):
        proc_ref[0, m] = gsum_f[m * REACH : (m + 1) * REACH]
        proc_ref[1, m] = gsum_c[m * REACH : (m + 1) * REACH]
    hgrad_ref[0] = gsum_c[head_at : head_at + 4]
    hgrad_ref[1] = gsum_c[head_at + 8 : head_at + 12]
    for copy in started:
        copy.wait_send()


def per_device(dims, node_input, fnb, few, parent, restrict, prolong, cnb, cew, ft, ct, w, head):
    D, S, H = dims
    L = S * H
    rows, width = node_input.shape
    coarse = ct.shape[1]
    flat = [a.reshape(1, rows) for a in (parent, restrict, prolong)]
    arguments = [node_input, fnb, few, *flat, cnb, cew, ft, ct, w, head]
    cap = 2 * rows // D
    blk = min(256, cap)
    nblk = 2 * rows // blk
    fb, cb = rows // REACH, coarse // REACH
    vm = pltpu.VMEM
    def sums(count):
        share = -(-count // (16 * L)) * 16
        return [
            vm((L * share, width), F32),
            vm((L, share, width), BF),
            vm((L, share, width), BF),
            vm((D, share, width), BF),
            vm((L, share, width), BF),
        ]

    scratch = [vm(a.shape, a.dtype) for a in arguments]
    scratch += [
        pltpu.SemaphoreType.DMA((12,)),
        vm((fb, 3 * REACH, REACH), BF),
        vm((cb, 3 * REACH, REACH), BF),
        vm((nblk, blk, rows), BF),
        vm((nblk, coarse, blk), BF),
        vm((nblk, coarse, blk), BF),
        vm((width, rows + 2 * REACH), BF),
        vm((width, coarse + 2 * REACH), BF),
        vm((2, REACH, width), BF),
        vm((2, width, REACH), BF),
        vm((2, width, REACH), BF),
        vm((2, width, REACH), BF),
        vm((2, width, REACH), BF),
        vm((2, width, REACH), BF),
        vm((2, width, REACH), BF),
        vm((8, rows), F32),
        vm((nblk, 8, blk), F32),
        vm((nblk, 8, blk), F32),
        vm((nblk, width, blk), BF),
        vm((nblk, width, blk), BF),
        vm((nblk, width, blk), BF),
        vm((nblk, width, blk), BF),
        vm((nblk, width, blk), BF),
        vm((width, rows), BF),
        vm((width, rows), BF),
        vm((width, rows), F32),
        vm((width, coarse), BF),
        vm((width, coarse), BF),
        vm((width, coarse), F32),
        vm((width, rows), F32),
        vm((width, rows), BF),
        vm((width, rows), BF),
        vm((width, coarse), BF),
        vm((width, coarse), F32),
        vm((2, 8, width), F32),
        *sums(3 * REACH),
        *sums(3 * REACH + 16),
        pltpu.SemaphoreType.DMA((4, 2)),
        pltpu.SemaphoreType.DMA((4, 2)),
        pltpu.SemaphoreType.DMA((5, D)),
        pltpu.SemaphoreType.DMA((5, D)),
        pltpu.SemaphoreType.DMA((4, L)),
        pltpu.SemaphoreType.DMA((4, L)),
    ]
    spec = pl.BlockSpec(memory_space=pltpu.VMEM)
    return pl.pallas_call(
        functools.partial(entry, dims),
        out_shape=(
            jax.ShapeDtypeStruct((rows, width), F32),
            jax.ShapeDtypeStruct((2, 3, width, width), F32),
            jax.ShapeDtypeStruct((2, 4, width), F32),
        ),
        in_specs=[pl.BlockSpec(memory_space=pl.ANY)] * 12,
        out_specs=(spec, spec, spec),
        scratch_shapes=scratch,
        compiler_params=pltpu.CompilerParams(
            collective_id=0, has_side_effects=True, vmem_limit_bytes=62 * 1024 * 1024
        ),
    )(*arguments)


def solution(mesh):
    dims = (mesh.shape["dom"], mesh.shape["sub"], mesh.shape["chip"])
    nodes = ("groups", "dom", "sub", "chip")
    return jax.shard_map(
        functools.partial(per_device, dims),
        mesh=mesh,
        in_specs=(
            P(nodes, None),
            P(None, nodes),
            P(None, nodes),
            P(nodes),
            P(nodes),
            P(nodes),
            P(None, nodes),
            P(None, nodes),
            P(None, nodes),
            P(None, nodes),
            P(),
            P(),
        ),
        out_specs=(
            P(nodes, None),
            P("groups", None, None, None),
            P("groups", None, None),
        ),
        check_vma=False,
    )
```
